512 devices in a mesh: row: 32 (over z_hi, x, core), col: 16 (over z_lo, y).
Axes of the slice: x: 4, y: 8, z: 8 (z_hi: 4, z_lo: 2; z = z_hi * 2 + z_lo), core: 2. Of those that a mesh axis runs over, the one named last changes fastest.
Arguments:
- noise: bfloat16 [16384, 2048], P('row', 'col'), may hold values from -10 to 10, as said below
- data: bfloat16 [2048, 16384], P('row', 'col'), may hold values from -10 to 10, as said below
Outputs:
- targets: bfloat16 [2048, 16384], P('col', 'row')
- row_potential: float32 [16384], P('row')
- col_potential: float32 [16384], P('col')
The draws below stay inside these ranges and needn't reach their ends.
Inputs may be any that keep to these rules, and one draw needn't show every extreme that they name: `noise`: entries of order one. `data`: entries of order one.
All inputs are finite; a program needn't handle non-finite values.
Results may differ from the reference program's by a relative error of at most 0.0049.
Values may be sent and summed in bfloat16 or wider, within the bound.
No kernel may reach another device: no remote copies, remote signals or barrier semaphores. Data moves between devices by JAX's collectives and lax.ppermute only.
A program may use at most 64 MiB of HBM per device.

```python
import math
import jax
import jax.numpy as jnp
from jax import lax

W = 2048
ITERS = 4
NR = 16384
NC = 16384


def draw_noise(key, part):
    key = jax.random.fold_in(key, 1)
    values = jnp.clip(jax.random.normal(key, (NR, W), jnp.float32), -5.0, 5.0)
    return values.astype(jnp.bfloat16)


def draw_data(key, part):
    key = jax.random.fold_in(key, 5)
    values = jnp.clip(jax.random.normal(key, (W, NC), jnp.float32), -5.0, 5.0)
    return values.astype(jnp.bfloat16)


def setup_inputs(seed: int = 0) -> dict:
    streams_of = jax.random.split(jax.random.key(seed), 3)
    return {
        "noise": draw_noise(jax.random.fold_in(streams_of[2], 71), 0),
        "data": draw_data(jax.random.fold_in(streams_of[2], 71), 0),
    }


EPS = 0.01


def log_sum(scores, axis):
    peak = jnp.max(scores, axis=axis, keepdims=True)
    total = jnp.sum(jnp.exp(scores - peak), axis=axis)
    return jnp.squeeze(peak, axis) + jnp.log(total)


def reference(noise, data):
    block = math.gcd(NR, 1024)
    count = NR // block
    noise_sq = jnp.sum(noise.astype(jnp.float32) ** 2, axis=1)
    data_sq = jnp.sum(data.astype(jnp.float32) ** 2, axis=0)
    cross = jnp.dot(noise, data, preferred_element_type=jnp.float32)
    cost = (noise_sq[:, None] + data_sq[None, :] - 2.0 * cross) / W
    blocks = cost.reshape(count, block, NC)
    col_potential = jnp.zeros((NC,), jnp.float32)
    row_potential = jnp.zeros((NR,), jnp.float32)
    for step in range(ITERS):
        def row_part(tile):
            return log_sum((col_potential[None, :] - tile) / EPS, 1)

        row_lse = lax.map(row_part, blocks).reshape(NR)
        row_potential = -EPS * jnp.log(float(NR)) - EPS * row_lse

        def col_part(pair):
            tile, pot = pair
            scores = (pot[:, None] - tile) / EPS
            peak = jnp.max(scores, axis=0)
            return peak, jnp.sum(jnp.exp(scores - peak[None, :]), axis=0)

        peaks, totals = lax.map(col_part, (blocks, row_potential.reshape(count, block)))
        whole_peak = jnp.max(peaks, axis=0)
        whole_total = jnp.sum(totals * jnp.exp(peaks - whole_peak[None, :]), axis=0)
        col_potential = -EPS * jnp.log(float(NC)) - EPS * (whole_peak + jnp.log(whole_total))

    def target_part(pair):
        tile, pot = pair
        weights = (NR * jnp.exp((pot[:, None] + col_potential[None, :] - tile) / EPS)).astype(jnp.bfloat16)
        return jnp.dot(data, weights.T, preferred_element_type=jnp.float32).astype(jnp.bfloat16)

    pieces = lax.map(target_part, (blocks, row_potential.reshape(count, block)))
    targets = jnp.transpose(pieces, (1, 0, 2)).reshape(W, NR)
    return targets, row_potential, col_potential
```

```python
import jax
import jax.numpy as jnp
from jax import lax
from jax.sharding import PartitionSpec as P

ITERS = 4

EPS = 0.01
LIFT = 64


def share(part, axis):
    copies = jnp.broadcast_to(part[None], (lax.axis_size(axis),) + part.shape)
    return lax.all_to_all(copies, axis, 0, 0)


def log_total(scores, dim, axis):
    peak = jnp.max(scores, axis=dim)
    total = jnp.sum(jnp.exp(scores - jnp.expand_dims(peak, dim)), axis=dim)
    both = share(jnp.stack([peak, total]), axis)
    peaks, totals = both[:, 0], both[:, 1]
    whole = jnp.max(peaks, axis=0)
    return whole + jnp.log(jnp.sum(totals * jnp.exp(peaks - whole[None]), axis=0))


def local(noise, data):
    width = noise.shape[1] * lax.axis_size("col")
    rows_all = noise.shape[0] * lax.axis_size("row")
    cols_all = data.shape[1] * lax.axis_size("col")
    data_full = lax.all_gather(data, "row", axis=0, tiled=True)
    noise_full = share(noise, "col").transpose(1, 0, 2).reshape(noise.shape[0], width)
    noise_sq = jnp.sum(noise_full.astype(jnp.float32) ** 2, axis=1)
    data_sq = jnp.sum(data_full.astype(jnp.float32) ** 2, axis=0)
    cross = jnp.dot(noise_full, data_full, preferred_element_type=jnp.float32)
    cost = (noise_sq[:, None] + data_sq[None, :] - 2.0 * cross) / width

    row_first = -EPS * jnp.log(float(rows_all)) - EPS * log_total(-cost / EPS, 1, "col")
    scores = (row_first[:, None] - cost) / EPS
    col_first = -EPS * jnp.log(float(cols_all)) - EPS * log_total(scores, 0, "row")

    lift = 2.0**LIFT
    plan = lift * jnp.exp((row_first[:, None] + col_first[None, :] - cost) / EPS)
    by_col = jnp.ones((data.shape[1],), jnp.float32)
    for step in range(1, ITERS):
        part = jnp.sum(plan * by_col[None, :], axis=1)
        by_row = (lift / rows_all) / jnp.sum(share(part, "col"), axis=0)
        part = jnp.sum(plan * by_row[:, None], axis=0)
        by_col = (lift / cols_all) / jnp.sum(share(part, "row"), axis=0)
    row_potential = row_first + EPS * jnp.log(by_row)
    col_potential = col_first + EPS * jnp.log(by_col)

    weights = (plan * ((rows_all / lift) * by_row)[:, None] * by_col[None, :]).astype(
        jnp.bfloat16
    )
    contract = (((1,), (1,)), ((), ()))
    terms = lax.dot_general(data_full, weights, contract, preferred_element_type=jnp.float32)
    n = lax.axis_size("col")
    terms = terms.astype(jnp.bfloat16).reshape(n, width // n, noise.shape[0])
    parts = lax.all_to_all(terms, "col", 0, 0)
    targets = jnp.sum(parts.astype(jnp.float32), axis=0).astype(jnp.bfloat16)
    return (targets, row_potential, col_potential)


def solution(mesh):
    placed = (P("row", "col"), P("row", "col"))
    return jax.shard_map(
        local,
        mesh=mesh,
        in_specs=placed,
        out_specs=(P("col", "row"), P("row"), P("col")),
        check_vma=False,
    )
```

```python
import jax
import jax.numpy as jnp
from jax import lax
from jax.sharding import PartitionSpec as P

ITERS = 4

EPS = 0.01
LIFT = 64

Z_HI, X, CORE = 4, 4, 2
Z_LO, Y = 2, 8
Y_GROUPS = [[z * Y + y for y in range(Y)] for z in range(Z_LO)]
OWNERS = [[z * Y + y for y in range(Y) for z in range(Z_LO)]]


def along_z(array, by):
    step = X * CORE
    pairs = [(i, (i + by * step) % (Z_HI * step)) for i in range(Z_HI * step)]
    return lax.ppermute(array, "row", pairs)


def along_x(array, by):
    step = X * CORE
    pairs = [(i, i // step * step + (i + by * CORE) % step) for i in range(Z_HI * step)]
    return lax.ppermute(array, "row", pairs)


def other_core(array):
    return lax.ppermute(array, "row", [(i, i ^ 1) for i in range(Z_HI * X * CORE)])


def other_z(array):
    return lax.ppermute(array, "col", [(i, (i + Y) % (Z_LO * Y)) for i in range(Z_LO * Y)])


def share(part, axis, groups=None):
    count = len(groups[0]) if groups else lax.axis_size(axis)
    copies = jnp.broadcast_to(part[None], (count,) + part.shape)
    return lax.all_to_all(copies, axis, 0, 0, axis_index_groups=groups)


def gather_noise(noise):
    there = other_z(noise)
    first = lax.axis_index("col") < Y
    low, high = jnp.where(first, noise, there), jnp.where(first, there, noise)
    half = noise.shape[1] // 2
    halves = [
        jnp.concatenate([low[:, k : k + half], high[:, k : k + half]], axis=1)
        for k in (0, half)
    ]
    return share(jnp.stack(halves), "col", Y_GROUPS)


def gather_data(data):
    row = lax.axis_index("row")
    z, x = row // (X * CORE), row // CORE % X
    up, down = along_z(data, 1), along_z(data, -1)
    far = along_z(up, 1)
    plane = jnp.zeros((2, Z_LO) + data.shape, data.dtype)
    for piece, by in ((data, 0), (up, 3), (down, 1), (far, 2)):
        at = (z + by) % Z_HI
        plane = lax.dynamic_update_slice(plane, piece[None, None], (at % 2, at // 2, 0, 0))
    up, down = along_x(plane, 1), along_x(plane, -1)
    far = along_x(up, 1)
    whole = jnp.zeros((2, X, Z_LO) + data.shape, data.dtype)
    for piece, by in ((plane, 0), (up, 3), (down, 1), (far, 2)):
        whole = lax.dynamic_update_slice(whole, piece[:, None], (0, (x + by) % X, 0, 0, 0))
    return whole.reshape(-1, data.shape[1])


def log_total(scores, dim, axis):
    peak = jnp.max(scores, axis=dim)
    total = jnp.sum(jnp.exp(scores - jnp.expand_dims(peak, dim)), axis=dim)
    logs = share(peak + jnp.log(total), axis)
    whole = jnp.max(logs, axis=0)
    return whole + jnp.log(jnp.sum(jnp.exp(logs - whole[None]), axis=0))


def local(noise, data):
    rows, cols = noise.shape[0], data.shape[1]
    width = noise.shape[1] * lax.axis_size("col")
    rows_all = rows * lax.axis_size("row")
    cols_all = cols * lax.axis_size("col")
    core = lax.axis_index("row") % CORE

    noise_all = gather_noise(noise)
    here = gather_data(data)
    there = other_core(here)
    sq = jnp.sum(here.astype(jnp.float32) ** 2, axis=0)
    data_sq = sq + other_core(sq)
    noise_sq = jnp.sum(noise_all.astype(jnp.float32) ** 2, axis=(0, 1, 3))

    def half(which):
        part = lax.dynamic_index_in_dim(noise_all, which, 1, keepdims=False)
        return part.transpose(1, 0, 2).reshape(rows, -1)

    cross = jnp.dot(half(core), here, preferred_element_type=jnp.float32)
    cross += jnp.dot(half(1 - core), there, preferred_element_type=jnp.float32)

    unit = 1.0 / (width * EPS)
    logits = cross * (2.0 * unit)
    row_first = -jnp.log(float(rows_all)) - log_total(
        logits - (data_sq * unit)[None, :], 1, "col"
    )
    col_first = -jnp.log(float(cols_all)) - log_total(logits + row_first[:, None], 0, "row")

    lift = 2.0**LIFT
    plan = lift * jnp.exp(logits + row_first[:, None] + col_first[None, :])
    by_col = jnp.ones((cols,), jnp.float32)
    for step in range(1, ITERS):
        part = jnp.sum(plan * by_col[None, :], axis=1)
        by_row = (lift / rows_all) / jnp.sum(share(part, "col"), axis=0)
        part = jnp.sum(plan * by_row[:, None], axis=0)
        by_col = (lift / cols_all) / jnp.sum(share(part, "row"), axis=0)
    row_potential = noise_sq / width + EPS * (row_first + jnp.log(by_row))
    col_potential = data_sq / width + EPS * (col_first + jnp.log(by_col))

    weights = (plan * ((rows_all / lift) * by_row)[:, None] * by_col[None, :]).astype(
        jnp.bfloat16
    )
    contract = (((1,), (1,)), ((), ()))
    terms = [
        lax.dot_general(part, weights, contract, preferred_element_type=jnp.float32)
        .astype(jnp.bfloat16)
        .reshape(Z_LO * Y, -1, rows)
        for part in (here, there)
    ]
    parts = lax.all_to_all(jnp.stack(terms, axis=1), "col", 0, 0, axis_index_groups=OWNERS)
    targets = jnp.sum(parts.astype(jnp.float32), axis=0).astype(jnp.bfloat16)
    targets = jnp.where(core == 0, targets, targets[::-1]).reshape(-1, rows)
    return (targets, row_potential, col_potential)


def solution(mesh):
    placed = (P("row", "col"), P("row", "col"))
    return jax.shard_map(
        local,
        mesh=mesh,
        in_specs=placed,
        out_specs=(P("col", "row"), P("row"), P("col")),
        check_vma=False,
    )
```

```python
import jax
import jax.numpy as jnp
from jax import lax
from jax.sharding import PartitionSpec as P

ITERS = 4

EPS = 0.01
LIFT = 64

Z_HI, X, CORE = 4, 4, 2
Z_LO, Y = 2, 8
PARITIES = [[z * Y + y + q for z in range(Z_LO) for y in range(0, Y, 2)] for q in range(2)]


def along_z(array, by):
    step = X * CORE
    pairs = [(i, (i + by * step) % (Z_HI * step)) for i in range(Z_HI * step)]
    return lax.ppermute(array, "row", pairs)


def along_x(array, by):
    step = X * CORE
    pairs = [(i, i // step * step + (i + by * CORE) % step) for i in range(Z_HI * step)]
    return lax.ppermute(array, "row", pairs)


def other_core(array):
    return lax.ppermute(array, "row", [(i, i ^ 1) for i in range(Z_HI * X * CORE)])


def neighbour(array, by):
    pairs = [
        (z * Y + y, z * Y + (y + (by if y % 2 == 0 else -by)) % Y)
        for z in range(Z_LO)
        for y in range(Y)
    ]
    return lax.ppermute(array, "col", pairs)


def share(part, axis, groups=None):
    count = len(groups[0]) if groups else lax.axis_size(axis)
    copies = jnp.broadcast_to(part[None], (count,) + part.shape)
    return lax.all_to_all(copies, axis, 0, 0, axis_index_groups=groups)


def gather_data(data):
    row = lax.axis_index("row")
    z, x = row // (X * CORE), row // CORE % X
    up, down = along_z(data, 1), along_z(data, -1)
    far = along_z(up, 1)
    plane = jnp.zeros((Z_HI,) + data.shape, data.dtype)
    for piece, by in ((data, 0), (up, 3), (down, 1), (far, 2)):
        plane = lax.dynamic_update_slice(plane, piece[None], ((z + by) % Z_HI, 0, 0))
    up, down = along_x(plane, 1), along_x(plane, -1)
    far = along_x(up, 1)
    whole = jnp.zeros((Z_HI, X) + data.shape, data.dtype)
    for piece, by in ((plane, 0), (up, 3), (down, 1), (far, 2)):
        whole = lax.dynamic_update_slice(whole, piece[:, None], (0, (x + by) % X, 0, 0))
    return whole


def log_total(scores, dim, axis):
    peak = jnp.max(scores, axis=dim)
    total = jnp.sum(jnp.exp(scores - jnp.expand_dims(peak, dim)), axis=dim)
    logs = share(peak + jnp.log(total), axis)
    whole = jnp.max(logs, axis=0)
    return whole + jnp.log(jnp.sum(jnp.exp(logs - whole[None]), axis=0))


def local(noise, data):
    rows, cols = noise.shape[0], data.shape[1]
    width = noise.shape[1] * lax.axis_size("col")
    rows_all = rows * lax.axis_size("row")
    cols_all = cols * lax.axis_size("col")
    core = lax.axis_index("row") % CORE

    noise_all = share(noise, "col")
    here = gather_data(data)
    there = other_core(here)
    sq = jnp.sum(here.astype(jnp.float32) ** 2, axis=(0, 1, 2))
    data_sq = sq + other_core(sq)
    noise_sq = jnp.sum(noise_all.astype(jnp.float32) ** 2, axis=(0, 2))

    def half(which):
        size = noise.shape[1] // CORE
        part = noise_all[:, :, which * size : (which + 1) * size]
        part = jnp.concatenate([part[0::2], part[1::2]], axis=2)
        return part.transpose(1, 0, 2).reshape(rows, -1)

    first, second = half(0), half(1)
    mine = jnp.where(core == 0, first, second)
    others = jnp.where(core == 0, second, first)
    cross = jnp.dot(mine, here.reshape(-1, cols), preferred_element_type=jnp.float32)
    cross += jnp.dot(others, there.reshape(-1, cols), preferred_element_type=jnp.float32)

    unit = 1.0 / (width * EPS)
    logits = cross * (2.0 * unit)
    row_first = -jnp.log(float(rows_all)) - log_total(
        logits - (data_sq * unit)[None, :], 1, "col"
    )
    col_first = -jnp.log(float(cols_all)) - log_total(logits + row_first[:, None], 0, "row")

    lift = 2.0**LIFT
    plan = lift * jnp.exp(logits + row_first[:, None] + col_first[None, :])
    by_col = jnp.ones((cols,), jnp.float32)
    for step in range(1, ITERS):
        part = jnp.sum(plan * by_col[None, :], axis=1)
        by_row = (lift / rows_all) / jnp.sum(share(part, "col"), axis=0)
        part = jnp.sum(plan * by_row[:, None], axis=0)
        by_col = (lift / cols_all) / jnp.sum(share(part, "row"), axis=0)
    row_potential = noise_sq / width + EPS * (row_first + jnp.log(by_row))
    col_potential = data_sq / width + EPS * (col_first + jnp.log(by_col))

    weights = (plan * ((rows_all / lift) * by_row)[:, None] * by_col[None, :]).astype(
        jnp.bfloat16
    )

    def features(parity):
        shape = (Z_HI, X // 2, 2, -1, cols)
        a = lax.dynamic_index_in_dim(here.reshape(shape), parity, 2, keepdims=False)
        b = lax.dynamic_index_in_dim(there.reshape(shape), parity, 2, keepdims=False)
        both = [jnp.where(core == 0, a, b), jnp.where(core == 0, b, a)]
        return jnp.stack(both, axis=2).reshape(Z_LO, -1, cols)

    def terms(part):
        contract = (((1,), (1,)), ((), ()))
        return lax.dot_general(part, weights, contract, preferred_element_type=jnp.float32)

    odd = lax.axis_index("col") % 2
    away, kept = features(1 - odd), features(odd)
    sums = [
        (terms(kept[z]) + neighbour(terms(away[z]).astype(jnp.bfloat16), by)).astype(
            jnp.bfloat16
        )
        for z, by in ((0, 1), (1, -1))
    ]
    sums = jnp.stack(sums).reshape(len(PARITIES[0]), -1, rows)
    parts = lax.all_to_all(sums, "col", 0, 0, axis_index_groups=PARITIES)
    targets = jnp.sum(parts.astype(jnp.float32), axis=0).astype(jnp.bfloat16)
    return (targets, row_potential, col_potential)


def solution(mesh):
    placed = (P("row", "col"), P("row", "col"))
    return jax.shard_map(
        local,
        mesh=mesh,
        in_specs=placed,
        out_specs=(P("col", "row"), P("row"), P("col")),
        check_vma=False,
    )
```

```python
import jax
import jax.numpy as jnp
from jax import lax
from jax.sharding import PartitionSpec as P

ITERS = 4

EPS = 0.01
LIFT = 64

Z_HI, X, CORE = 4, 4, 2
Z_LO, Y = 2, 8
PARITIES = [[z * Y + y + q for z in range(Z_LO) for y in range(0, Y, 2)] for q in range(2)]


def along_z(array, by):
    step = X * CORE
    pairs = [(i, (i + by * step) % (Z_HI * step)) for i in range(Z_HI * step)]
    return lax.ppermute(array, "row", pairs)


def along_x(array, by):
    step = X * CORE
    pairs = [(i, i // step * step + (i + by * CORE) % step) for i in range(Z_HI * step)]
    return lax.ppermute(array, "row", pairs)


def other_core(array):
    return lax.ppermute(array, "row", [(i, i ^ 1) for i in range(Z_HI * X * CORE)])


def neighbour(array, by):
    pairs = [
        (z * Y + y, z * Y + (y + (by if y % 2 == 0 else -by)) % Y)
        for z in range(Z_LO)
        for y in range(Y)
    ]
    return lax.ppermute(array, "col", pairs)


def share(part, axis, groups=None):
    count = len(groups[0]) if groups else lax.axis_size(axis)
    copies = jnp.broadcast_to(part[None], (count,) + part.shape)
    return lax.all_to_all(copies, axis, 0, 0, axis_index_groups=groups)


def gather(noise, data):
    row, odd = lax.axis_index("row"), lax.axis_index("col") % 2
    z, x = row // (X * CORE), row // CORE % X
    same = share(noise, "col", PARITIES)
    up, down, far = along_z(data, 1), along_z(data, -1), along_z(data, 2)
    plane = jnp.zeros((Z_HI,) + data.shape, data.dtype)
    for piece, by in ((data, 0), (up, 3), (down, 1), (far, 2)):
        plane = lax.dynamic_update_slice(plane, piece[None], ((z + by) % Z_HI, 0, 0))
    up, down = along_x(plane, 1), along_x(plane, -1)
    up, same = lax.optimization_barrier((up, same))
    far = along_x(up, 1)
    n = len(PARITIES[0])
    above, below = neighbour(same[: n // 2], 1), neighbour(same[n // 2 :], -1)
    far, above, below = lax.optimization_barrier((far, above, below))
    whole = jnp.zeros((Z_HI, X) + data.shape, data.dtype)
    for piece, by in ((plane, 0), (up, 3), (down, 1), (far, 2)):
        whole = lax.dynamic_update_slice(whole, piece[:, None], (0, (x + by) % X, 0, 0))
    other = jnp.concatenate([above, below])
    by_parity = [jnp.where(odd == 0, same, other), jnp.where(odd == 0, other, same)]
    return by_parity, whole


def log_total(scores, dim, axis):
    peak = jnp.max(scores, axis=dim)
    total = jnp.sum(jnp.exp(scores - jnp.expand_dims(peak, dim)), axis=dim)
    logs = share(peak + jnp.log(total), axis)
    whole = jnp.max(logs, axis=0)
    return whole + jnp.log(jnp.sum(jnp.exp(logs - whole[None]), axis=0))


def local(noise, data):
    rows, cols = noise.shape[0], data.shape[1]
    width = noise.shape[1] * lax.axis_size("col")
    rows_all = rows * lax.axis_size("row")
    cols_all = cols * lax.axis_size("col")
    core = lax.axis_index("row") % CORE

    by_parity, here = gather(noise, data)
    there = other_core(here)
    sq = jnp.sum(here.astype(jnp.float32) ** 2, axis=(0, 1, 2))
    data_sq = sq + other_core(sq)
    noise_sq = sum(jnp.sum(part.astype(jnp.float32) ** 2, axis=(0, 2)) for part in by_parity)

    def half(which):
        size = noise.shape[1] // CORE
        part = [p[:, :, which * size : (which + 1) * size] for p in by_parity]
        part = jnp.concatenate(part, axis=2)
        return part.transpose(1, 0, 2).reshape(rows, -1)

    first, second = half(0), half(1)
    mine = jnp.where(core == 0, first, second)
    others = jnp.where(core == 0, second, first)
    cross = jnp.dot(mine, here.reshape(-1, cols), preferred_element_type=jnp.float32)
    cross += jnp.dot(others, there.reshape(-1, cols), preferred_element_type=jnp.float32)

    unit = 1.0 / (width * EPS)
    logits = cross * (2.0 * unit)
    row_first = -jnp.log(float(rows_all)) - log_total(
        logits - (data_sq * unit)[None, :], 1, "col"
    )
    col_first = -jnp.log(float(cols_all)) - log_total(logits + row_first[:, None], 0, "row")

    lift = 2.0**LIFT
    plan = lift * jnp.exp(logits + row_first[:, None] + col_first[None, :])
    by_col = jnp.ones((cols,), jnp.float32)
    for step in range(1, ITERS):
        part = jnp.sum(plan * by_col[None, :], axis=1)
        by_row = (lift / rows_all) / jnp.sum(share(part, "col"), axis=0)
        part = jnp.sum(plan * by_row[:, None], axis=0)
        by_col = (lift / cols_all) / jnp.sum(share(part, "row"), axis=0)
    row_potential = noise_sq / width + EPS * (row_first + jnp.log(by_row))
    col_potential = data_sq / width + EPS * (col_first + jnp.log(by_col))

    weights = (plan * ((rows_all / lift) * by_row)[:, None] * by_col[None, :]).astype(
        jnp.bfloat16
    )

    def features(parity):
        shape = (Z_HI, X // 2, 2, -1, cols)
        a = lax.dynamic_index_in_dim(here.reshape(shape), parity, 2, keepdims=False)
        b = lax.dynamic_index_in_dim(there.reshape(shape), parity, 2, keepdims=False)
        both = [jnp.where(core == 0, a, b), jnp.where(core == 0, b, a)]
        return jnp.stack(both, axis=2).reshape(Z_LO, -1, cols)

    def terms(part):
        contract = (((1,), (1,)), ((), ()))
        return lax.dot_general(part, weights, contract, preferred_element_type=jnp.float32)

    odd = lax.axis_index("col") % 2
    away, kept = features(1 - odd), features(odd)
    sums = [
        (terms(kept[z]) + neighbour(terms(away[z]).astype(jnp.bfloat16), by)).astype(
            jnp.bfloat16
        )
        for z, by in ((0, 1), (1, -1))
    ]
    sums = jnp.stack(sums).reshape(len(PARITIES[0]), -1, rows)
    parts = lax.all_to_all(sums, "col", 0, 0, axis_index_groups=PARITIES)
    targets = jnp.sum(parts.astype(jnp.float32), axis=0).astype(jnp.bfloat16)
    return (targets, row_potential, col_potential)


def solution(mesh):
    placed = (P("row", "col"), P("row", "col"))
    return jax.shard_map(
        local,
        mesh=mesh,
        in_specs=placed,
        out_specs=(P("col", "row"), P("row"), P("col")),
        check_vma=False,
    )
```

```python
import jax
import jax.numpy as jnp
from jax import lax
from jax.sharding import PartitionSpec as P

ITERS = 4

EPS = 0.01
LIFT = 64

Z_HI, X, CORE = 4, 4, 2
Z_LO, Y = 2, 8
PARITIES = [
    [z * Y + h * X + y + q for y in range(0, X, 2) for z in range(Z_LO) for h in range(Y // X)]
    for q in range(2)
]
LINES = [[(z * X + x) * CORE + c for x in range(X)] for z in range(Z_HI) for c in range(CORE)]


def along_z(array, by):
    step = X * CORE
    pairs = [(i, (i + by * step) % (Z_HI * step)) for i in range(Z_HI * step)]
    return lax.ppermute(array, "row", pairs)


def other_core(array):
    return lax.ppermute(array, "row", [(i, i ^ 1) for i in range(Z_HI * X * CORE)])


def neighbour(array, by):
    pairs = [
        (z * Y + y, z * Y + (y + (by if y % 2 == 0 else -by)) % Y)
        for z in range(Z_LO)
        for y in range(Y)
    ]
    return lax.ppermute(array, "col", pairs)


def share(part, axis, groups=None):
    count = len(groups[0]) if groups else lax.axis_size(axis)
    copies = jnp.broadcast_to(part[None], (count,) + part.shape)
    return lax.all_to_all(copies, axis, 0, 0, axis_index_groups=groups)


def gather(noise, data):
    row, odd = lax.axis_index("row"), lax.axis_index("col") % 2
    z = row // (X * CORE)
    same = share(noise, "col", PARITIES)
    plane = jnp.zeros((Z_HI,) + data.shape, data.dtype)
    pieces = (data, along_z(data, -1), along_z(data, 2), along_z(data, 1))
    for by, piece in enumerate(pieces):
        plane = lax.dynamic_update_slice(plane, piece[None], ((z + by) % Z_HI, 0, 0))
    plane, same = lax.optimization_barrier((plane, same))
    whole = share(plane, "row", LINES)
    n = len(PARITIES[0]) // 2
    above, below = neighbour(same[:n], 1), neighbour(same[n:], -1)
    whole, above, below = lax.optimization_barrier((whole, above, below))
    other = jnp.concatenate([above, below])
    by_parity = [jnp.where(odd == 0, same, other), jnp.where(odd == 0, other, same)]
    return by_parity, whole


def log_total(scores, dim, axis):
    peak = jnp.max(scores, axis=dim)
    total = jnp.sum(jnp.exp(scores - jnp.expand_dims(peak, dim)), axis=dim)
    logs = share(peak + jnp.log(total), axis)
    whole = jnp.max(logs, axis=0)
    return whole + jnp.log(jnp.sum(jnp.exp(logs - whole[None]), axis=0))


def local(noise, data):
    rows, cols = noise.shape[0], data.shape[1]
    width = noise.shape[1] * lax.axis_size("col")
    rows_all = rows * lax.axis_size("row")
    cols_all = cols * lax.axis_size("col")
    core = lax.axis_index("row") % CORE

    by_parity, here = gather(noise, data)
    there = other_core(here)
    sq = jnp.sum(here.astype(jnp.float32) ** 2, axis=(0, 1, 2))
    data_sq = sq + other_core(sq)
    noise_sq = sum(jnp.sum(part.astype(jnp.float32) ** 2, axis=(0, 2)) for part in by_parity)

    def half(which):
        size = noise.shape[1] // CORE
        part = [p[:, :, which * size : (which + 1) * size] for p in by_parity]
        part = [p.reshape((X // 2, -1) + p.shape[1:]) for p in part]
        return jnp.stack(part, axis=1).transpose(3, 0, 1, 2, 4).reshape(rows, -1)

    first, second = half(0), half(1)
    mine = jnp.where(core == 0, first, second)
    others = jnp.where(core == 0, second, first)
    cross = jnp.dot(mine, here.reshape(-1, cols), preferred_element_type=jnp.float32)
    cross += jnp.dot(others, there.reshape(-1, cols), preferred_element_type=jnp.float32)

    unit = 1.0 / (width * EPS)
    logits = cross * (2.0 * unit)
    row_first = -jnp.log(float(rows_all)) - log_total(
        logits - (data_sq * unit)[None, :], 1, "col"
    )
    col_first = -jnp.log(float(cols_all)) - log_total(logits + row_first[:, None], 0, "row")

    lift = 2.0**LIFT
    plan = lift * jnp.exp(logits + row_first[:, None] + col_first[None, :])
    by_col = jnp.ones((cols,), jnp.float32)
    for step in range(1, ITERS):
        part = jnp.sum(plan * by_col[None, :], axis=1)
        by_row = (lift / rows_all) / jnp.sum(share(part, "col"), axis=0)
        part = jnp.sum(plan * by_row[:, None], axis=0)
        by_col = (lift / cols_all) / jnp.sum(share(part, "row"), axis=0)
    row_potential = noise_sq / width + EPS * (row_first + jnp.log(by_row))
    col_potential = data_sq / width + EPS * (col_first + jnp.log(by_col))

    weights = (plan * ((rows_all / lift) * by_row)[:, None] * by_col[None, :]).astype(
        jnp.bfloat16
    )

    def features(parity):
        shape = (X // 2, 2, Z_HI, -1, cols)
        a = lax.dynamic_index_in_dim(here.reshape(shape), parity, 1, keepdims=False)
        b = lax.dynamic_index_in_dim(there.reshape(shape), parity, 1, keepdims=False)
        both = [jnp.where(core == 0, a, b), jnp.where(core == 0, b, a)]
        return jnp.stack(both, axis=2).reshape(X // 2, -1, cols)

    def terms(part):
        contract = (((1,), (1,)), ((), ()))
        return lax.dot_general(part, weights, contract, preferred_element_type=jnp.float32)

    odd = lax.axis_index("col") % 2
    away, kept = features(1 - odd), features(odd)
    sums = [
        (terms(kept[z]) + neighbour(terms(away[z]).astype(jnp.bfloat16), by)).astype(
            jnp.bfloat16
        )
        for z, by in ((0, 1), (1, -1))
    ]
    sums = jnp.stack(sums).reshape(len(PARITIES[0]), -1, rows)
    parts = lax.all_to_all(sums, "col", 0, 0, axis_index_groups=PARITIES)
    targets = jnp.sum(parts.astype(jnp.float32), axis=0).astype(jnp.bfloat16)
    return (targets, row_potential, col_potential)


def solution(mesh):
    placed = (P("row", "col"), P("row", "col"))
    return jax.shard_map(
        local,
        mesh=mesh,
        in_specs=placed,
        out_specs=(P("col", "row"), P("row"), P("col")),
        check_vma=False,
    )
```

```python
import jax
import jax.numpy as jnp
from jax import lax
from jax.sharding import PartitionSpec as P

ITERS = 4

EPS = 0.01
LIFT = 64

Z_HI, X, CORE = 4, 4, 2
Z_LO, Y = 2, 8
PARITIES = [
    [z * Y + h * X + y + q for y in range(0, X, 2) for z in range(Z_LO) for h in range(Y // X)]
    for q in range(2)
]
LINES = [[(z * X + x) * CORE + c for x in range(X)] for z in range(Z_HI) for c in range(CORE)]


def along_z(array, by):
    step = X * CORE
    pairs = [(i, (i + by * step) % (Z_HI * step)) for i in range(Z_HI * step)]
    return lax.ppermute(array, "row", pairs)


def other_core(array):
    return lax.ppermute(array, "row", [(i, i ^ 1) for i in range(Z_HI * X * CORE)])


def neighbour(array, by):
    pairs = [
        (z * Y + y, z * Y + (y + (by if y % 2 == 0 else -by)) % Y)
        for z in range(Z_LO)
        for y in range(Y)
    ]
    return lax.ppermute(array, "col", pairs)


def share(part, axis, groups=None):
    count = len(groups[0]) if groups else lax.axis_size(axis)
    copies = jnp.broadcast_to(part[None], (count,) + part.shape)
    return lax.all_to_all(copies, axis, 0, 0, axis_index_groups=groups)


def gather(noise, data):
    z = lax.axis_index("row") // (X * CORE)
    same = share(noise, "col", PARITIES)
    plane = jnp.zeros((Z_HI,) + data.shape, data.dtype)
    pieces = (data, along_z(data, -1), along_z(data, 2), along_z(data, 1))
    for by, piece in enumerate(pieces):
        plane = lax.dynamic_update_slice(plane, piece[None], ((z + by) % Z_HI, 0, 0))
    return lax.optimization_barrier((same, plane))


def log_total(scores, dim, axis):
    peak = jnp.max(scores, axis=dim)
    total = jnp.sum(jnp.exp(scores - jnp.expand_dims(peak, dim)), axis=dim)
    logs = share(peak + jnp.log(total), axis)
    whole = jnp.max(logs, axis=0)
    return whole + jnp.log(jnp.sum(jnp.exp(logs - whole[None]), axis=0))


def local(noise, data):
    rows, cols = noise.shape[0], data.shape[1]
    width = noise.shape[1] * lax.axis_size("col")
    rows_all = rows * lax.axis_size("row")
    cols_all = cols * lax.axis_size("col")
    core = lax.axis_index("row") % CORE

    odd = lax.axis_index("col") % 2

    same, plane = gather(noise, data)
    here = share(plane, "row", LINES)
    n = len(PARITIES[0]) // 2
    other = jnp.concatenate([neighbour(same[:n], 1), neighbour(same[n:], -1)])
    by_parity = [jnp.where(odd == 0, same, other), jnp.where(odd == 0, other, same)]
    noise_sq = sum(jnp.sum(part.astype(jnp.float32) ** 2, axis=(0, 2)) for part in by_parity)

    def half(which):
        size = noise.shape[1] // CORE
        part = [p[:, :, which * size : (which + 1) * size] for p in by_parity]
        part = [p.reshape((X // 2, -1) + p.shape[1:]) for p in part]
        return jnp.stack(part, axis=1).transpose(3, 0, 1, 2, 4).reshape(rows, -1)

    first, second = half(0), half(1)
    mine = jnp.where(core == 0, first, second)
    others = jnp.where(core == 0, second, first)
    here, mine, others, noise_sq, kept, away = lax.optimization_barrier(
        (here, mine, others, noise_sq, odd, 1 - odd)
    )
    there = other_core(here)
    sq = jnp.sum(here.astype(jnp.float32) ** 2, axis=(0, 1, 2))
    data_sq = sq + other_core(sq)
    cross = jnp.dot(mine, here.reshape(-1, cols), preferred_element_type=jnp.float32)
    cross += jnp.dot(others, there.reshape(-1, cols), preferred_element_type=jnp.float32)

    unit = 1.0 / (width * EPS)
    logits = cross * (2.0 * unit)
    row_first = -jnp.log(float(rows_all)) - log_total(
        logits - (data_sq * unit)[None, :], 1, "col"
    )
    col_first = -jnp.log(float(cols_all)) - log_total(logits + row_first[:, None], 0, "row")

    lift = 2.0**LIFT
    plan = lift * jnp.exp(logits + row_first[:, None] + col_first[None, :])
    by_col = jnp.ones((cols,), jnp.float32)
    for step in range(1, ITERS):
        part = jnp.sum(plan * by_col[None, :], axis=1)
        by_row = (lift / rows_all) / jnp.sum(share(part, "col"), axis=0)
        part = jnp.sum(plan * by_row[:, None], axis=0)
        by_col = (lift / cols_all) / jnp.sum(share(part, "row"), axis=0)
    weights = (plan * ((rows_all / lift) * by_row)[:, None] * by_col[None, :]).astype(
        jnp.bfloat16
    )

    def features(parity):
        shape = (X // 2, 2, Z_HI, -1, cols)
        a = lax.dynamic_index_in_dim(here.reshape(shape), parity, 1, keepdims=False)
        b = lax.dynamic_index_in_dim(there.reshape(shape), parity, 1, keepdims=False)
        both = [jnp.where(core == 0, a, b), jnp.where(core == 0, b, a)]
        return jnp.stack(both, axis=2).reshape(X // 2, -1, cols)

    def terms(part):
        contract = (((1,), (1,)), ((), ()))
        return lax.dot_general(part, weights, contract, preferred_element_type=jnp.float32)

    sent = [terms(part).astype(jnp.bfloat16) for part in features(away)]
    got = [neighbour(part, by) for part, by in zip(sent, (1, -1))]
    sent, kept, by_row, by_col = lax.optimization_barrier((sent[0], kept, by_row, by_col))
    row_potential = noise_sq / width + EPS * (row_first + jnp.log(by_row))
    col_potential = data_sq / width + EPS * (col_first + jnp.log(by_col))
    sums = [
        (terms(own) + add).astype(jnp.bfloat16) for own, add in zip(features(kept), got)
    ]
    sums = jnp.stack(sums).reshape(len(PARITIES[0]), -1, rows)
    parts = lax.all_to_all(sums, "col", 0, 0, axis_index_groups=PARITIES)
    targets = jnp.sum(parts.astype(jnp.float32), axis=0).astype(jnp.bfloat16)
    return (targets, row_potential, col_potential)


def solution(mesh):
    placed = (P("row", "col"), P("row", "col"))
    return jax.shard_map(
        local,
        mesh=mesh,
        in_specs=placed,
        out_specs=(P("col", "row"), P("row"), P("col")),
        check_vma=False,
    )
```

```python
import jax
import jax.numpy as jnp
from jax import lax
from jax.sharding import PartitionSpec as P

ITERS = 4

EPS = 0.01
LIFT = 64

Z_HI, X, CORE = 4, 4, 2
Z_LO, Y = 2, 8
PARITIES = [
    [z * Y + h * X + y + q for y in range(0, X, 2) for z in range(Z_LO) for h in range(Y // X)]
    for q in range(2)
]
LINES = [[(z * X + x) * CORE + c for x in range(X)] for z in range(Z_HI) for c in range(CORE)]


def along_z(array, by):
    step = X * CORE
    pairs = [(i, (i + by[i % CORE] * step) % (Z_HI * step)) for i in range(Z_HI * step)]
    return lax.ppermute(array, "row", pairs)


def other_core(array):
    return lax.ppermute(array, "row", [(i, i ^ 1) for i in range(Z_HI * X * CORE)])


def neighbour(array, by):
    pairs = [
        (z * Y + y, z * Y + (y + (by if y % 2 == 0 else -by)) % Y)
        for z in range(Z_LO)
        for y in range(Y)
    ]
    return lax.ppermute(array, "col", pairs)


def share(part, axis, groups=None):
    count = len(groups[0]) if groups else lax.axis_size(axis)
    copies = jnp.broadcast_to(part[None], (count,) + part.shape)
    return lax.all_to_all(copies, axis, 0, 0, axis_index_groups=groups)


def gather(noise, data):
    row = lax.axis_index("row")
    z, core = row // (X * CORE), row % CORE
    same = share(noise, "col", PARITIES)
    plane = jnp.zeros((Z_HI,) + data.shape, data.dtype)
    up, down = along_z(data, (1, 1)), along_z(data, (-1, -1))
    far = along_z(jnp.where(core == 0, up, down), (1, -1))
    for by, piece in enumerate((data, down, far, up)):
        plane = lax.dynamic_update_slice(plane, piece[None], ((z + by) % Z_HI, 0, 0))
    return lax.optimization_barrier((same, plane))


def log_total(scores, dim, axis):
    peak = jnp.max(scores, axis=dim)
    total = jnp.sum(jnp.exp(scores - jnp.expand_dims(peak, dim)), axis=dim)
    logs = share(peak + jnp.log(total), axis)
    whole = jnp.max(logs, axis=0)
    return whole + jnp.log(jnp.sum(jnp.exp(logs - whole[None]), axis=0))


def local(noise, data):
    rows, cols = noise.shape[0], data.shape[1]
    width = noise.shape[1] * lax.axis_size("col")
    rows_all = rows * lax.axis_size("row")
    cols_all = cols * lax.axis_size("col")
    core = lax.axis_index("row") % CORE

    odd = lax.axis_index("col") % 2

    same, plane = gather(noise, data)
    here = share(plane, "row", LINES)
    n = len(PARITIES[0]) // 2
    other = jnp.concatenate([neighbour(same[:n], 1), neighbour(same[n:], -1)])
    by_parity = [jnp.where(odd == 0, same, other), jnp.where(odd == 0, other, same)]
    noise_sq = sum(jnp.sum(part.astype(jnp.float32) ** 2, axis=(0, 2)) for part in by_parity)

    def half(which):
        size = noise.shape[1] // CORE
        part = [p[:, :, which * size : (which + 1) * size] for p in by_parity]
        part = [p.reshape((X // 2, -1) + p.shape[1:]) for p in part]
        return jnp.stack(part, axis=1).transpose(3, 0, 1, 2, 4).reshape(rows, -1)

    first, second = half(0), half(1)
    mine = jnp.where(core == 0, first, second)
    others = jnp.where(core == 0, second, first)
    here, mine, others, noise_sq, kept, away = lax.optimization_barrier(
        (here, mine, others, noise_sq, odd, 1 - odd)
    )
    there = other_core(here)
    sq = jnp.sum(here.astype(jnp.float32) ** 2, axis=(0, 1, 2))
    data_sq = sq + other_core(sq)
    cross = jnp.dot(mine, here.reshape(-1, cols), preferred_element_type=jnp.float32)
    cross += jnp.dot(others, there.reshape(-1, cols), preferred_element_type=jnp.float32)

    unit = 1.0 / (width * EPS)
    logits = cross * (2.0 * unit)
    row_first = -jnp.log(float(rows_all)) - log_total(
        logits - (data_sq * unit)[None, :], 1, "col"
    )
    col_first = -jnp.log(float(cols_all)) - log_total(logits + row_first[:, None], 0, "row")

    lift = 2.0**LIFT
    plan = lift * jnp.exp(logits + row_first[:, None] + col_first[None, :])
    by_col = jnp.ones((cols,), jnp.float32)
    for step in range(1, ITERS):
        part = jnp.sum(plan * by_col[None, :], axis=1)
        by_row = (lift / rows_all) / jnp.sum(share(part, "col"), axis=0)
        part = jnp.sum(plan * by_row[:, None], axis=0)
        by_col = (lift / cols_all) / jnp.sum(share(part, "row"), axis=0)
    row_potential = noise_sq / width + EPS * (row_first + jnp.log(by_row))
    col_potential = data_sq / width + EPS * (col_first + jnp.log(by_col))

    weights = (plan * ((rows_all / lift) * by_row)[:, None] * by_col[None, :]).astype(
        jnp.bfloat16
    )

    def features(parity):
        shape = (X // 2, 2, Z_HI, -1, cols)
        a = lax.dynamic_index_in_dim(here.reshape(shape), parity, 1, keepdims=False)
        b = lax.dynamic_index_in_dim(there.reshape(shape), parity, 1, keepdims=False)
        both = [jnp.where(core == 0, a, b), jnp.where(core == 0, b, a)]
        return jnp.stack(both, axis=2).reshape(X // 2, -1, cols)

    def terms(part):
        contract = (((1,), (1,)), ((), ()))
        return lax.dot_general(part, weights, contract, preferred_element_type=jnp.float32)

    sent = [terms(part).astype(jnp.bfloat16) for part in features(away)]
    got = [neighbour(part, by) for part, by in zip(sent, (1, -1))]
    sums = [
        (terms(own) + add).astype(jnp.bfloat16) for own, add in zip(features(kept), got)
    ]
    sums = jnp.stack(sums).reshape(len(PARITIES[0]), -1, rows)
    parts = lax.all_to_all(sums, "col", 0, 0, axis_index_groups=PARITIES)
    targets = jnp.sum(parts.astype(jnp.float32), axis=0).astype(jnp.bfloat16)
    return (targets, row_potential, col_potential)


def solution(mesh):
    placed = (P("row", "col"), P("row", "col"))
    return jax.shard_map(
        local,
        mesh=mesh,
        in_specs=placed,
        out_specs=(P("col", "row"), P("row"), P("col")),
        check_vma=False,
    )
```

```python
import jax
import jax.numpy as jnp
from jax import lax
from jax.sharding import PartitionSpec as P

ITERS = 4

EPS = 0.01
LIFT = 64

Z_HI, X, CORE = 4, 4, 2
Z_LO, Y = 2, 8
PARITIES = [
    [z * Y + h * X + y + q for y in range(0, X, 2) for z in range(Z_LO) for h in range(Y // X)]
    for q in range(2)
]
LINES = [[(z * X + x) * CORE + c for x in range(X)] for z in range(Z_HI) for c in range(CORE)]


def along_z(array, by):
    step = X * CORE
    pairs = [(i, (i + by * step) % (Z_HI * step)) for i in range(Z_HI * step)]
    return lax.ppermute(array, "row", pairs)


def other_core(array):
    return lax.ppermute(array, "row", [(i, i ^ 1) for i in range(Z_HI * X * CORE)])


def neighbour(array, by):
    pairs = [
        (z * Y + y, z * Y + (y + (by if y % 2 == 0 else -by)) % Y)
        for z in range(Z_LO)
        for y in range(Y)
    ]
    return lax.ppermute(array, "col", pairs)


def share(part, axis, groups=None):
    count = len(groups[0]) if groups else lax.axis_size(axis)
    copies = jnp.broadcast_to(part[None], (count,) + part.shape)
    return lax.all_to_all(copies, axis, 0, 0, axis_index_groups=groups)


def gather(noise, data):
    z = lax.axis_index("row") // (X * CORE)
    same = share(noise, "col", PARITIES)
    plane = jnp.zeros((Z_HI,) + data.shape, data.dtype)
    pieces = (data, along_z(data, -1), along_z(data, 2), along_z(data, 1))
    for by, piece in enumerate(pieces):
        plane = lax.dynamic_update_slice(plane, piece[None], ((z + by) % Z_HI, 0, 0))
    return lax.optimization_barrier((same, plane))


def log_total(scores, dim, axis):
    peak = jnp.max(scores, axis=dim)
    total = jnp.sum(jnp.exp(scores - jnp.expand_dims(peak, dim)), axis=dim)
    logs = share(peak + jnp.log(total), axis)
    whole = jnp.max(logs, axis=0)
    return whole + jnp.log(jnp.sum(jnp.exp(logs - whole[None]), axis=0))


def local(noise, data):
    rows, cols = noise.shape[0], data.shape[1]
    width = noise.shape[1] * lax.axis_size("col")
    rows_all = rows * lax.axis_size("row")
    cols_all = cols * lax.axis_size("col")
    core = lax.axis_index("row") % CORE

    odd = lax.axis_index("col") % 2

    same, plane = gather(noise, data)
    here = share(plane, "row", LINES)
    n = len(PARITIES[0]) // 2
    halves = [neighbour(same[:n], 1), neighbour(same[n:], -1)]
    other = jnp.concatenate(halves)
    by_parity = [jnp.where(odd == 0, same, other), jnp.where(odd == 0, other, same)]
    noise_sq = sum(jnp.sum(part.astype(jnp.float32) ** 2, axis=(0, 2)) for part in by_parity)

    def half(which):
        size = noise.shape[1] // CORE
        part = [p[:, :, which * size : (which + 1) * size] for p in by_parity]
        part = [p.reshape((X // 2, -1) + p.shape[1:]) for p in part]
        return jnp.stack(part, axis=1).transpose(3, 0, 1, 2, 4).reshape(rows, -1)

    first, second = half(0), half(1)
    mine = jnp.where(core == 0, first, second)
    others = jnp.where(core == 0, second, first)
    here, _, kept, away = lax.optimization_barrier((here, halves, odd, 1 - odd))
    there = other_core(here)
    squares = [jnp.sum(part.astype(jnp.float32) ** 2, axis=(0, 1, 2)) for part in (here, there)]
    data_sq = sum(lax.optimization_barrier(squares))
    cross = jnp.dot(mine, here.reshape(-1, cols), preferred_element_type=jnp.float32)
    cross += jnp.dot(others, there.reshape(-1, cols), preferred_element_type=jnp.float32)

    unit = 1.0 / (width * EPS)
    logits = cross * (2.0 * unit)
    row_first = -jnp.log(float(rows_all)) - log_total(
        logits - (data_sq * unit)[None, :], 1, "col"
    )
    col_first = -jnp.log(float(cols_all)) - log_total(logits + row_first[:, None], 0, "row")

    lift = 2.0**LIFT
    plan = lift * jnp.exp(logits + row_first[:, None] + col_first[None, :])
    by_col = jnp.ones((cols,), jnp.float32)
    for step in range(1, ITERS):
        part = jnp.sum(plan * by_col[None, :], axis=1)
        by_row = (lift / rows_all) / jnp.sum(share(part, "col"), axis=0)
        part = jnp.sum(plan * by_row[:, None], axis=0)
        by_col = (lift / cols_all) / jnp.sum(share(part, "row"), axis=0)
    row_potential = noise_sq / width + EPS * (row_first + jnp.log(by_row))
    col_potential = data_sq / width + EPS * (col_first + jnp.log(by_col))

    weights = (plan * ((rows_all / lift) * by_row)[:, None] * by_col[None, :]).astype(
        jnp.bfloat16
    )

    def features(parity):
        shape = (X // 2, 2, Z_HI, -1, cols)
        a = lax.dynamic_index_in_dim(here.reshape(shape), parity, 1, keepdims=False)
        b = lax.dynamic_index_in_dim(there.reshape(shape), parity, 1, keepdims=False)
        both = [jnp.where(core == 0, a, b), jnp.where(core == 0, b, a)]
        return jnp.stack(both, axis=2).reshape(X // 2, -1, cols)

    def terms(part):
        contract = (((1,), (1,)), ((), ()))
        return lax.dot_general(part, weights, contract, preferred_element_type=jnp.float32)

    sent = [terms(part).astype(jnp.bfloat16) for part in features(away)]
    got = [neighbour(part, by) for part, by in zip(sent, (1, -1))]
    sums = [
        (terms(own) + add).astype(jnp.bfloat16) for own, add in zip(features(kept), got)
    ]
    sums = jnp.stack(sums).reshape(len(PARITIES[0]), -1, rows)
    parts = lax.all_to_all(sums, "col", 0, 0, axis_index_groups=PARITIES)
    targets = jnp.sum(parts.astype(jnp.float32), axis=0).astype(jnp.bfloat16)
    return (targets, row_potential, col_potential)


def solution(mesh):
    placed = (P("row", "col"), P("row", "col"))
    return jax.shard_map(
        local,
        mesh=mesh,
        in_specs=placed,
        out_specs=(P("col", "row"), P("row"), P("col")),
        check_vma=False,
    )
```

```python
import jax
import jax.numpy as jnp
from jax import lax
from jax.sharding import PartitionSpec as P

ITERS = 4

EPS = 0.01
LIFT = 64

Z_HI, X, CORE = 4, 4, 2
Z_LO, Y = 2, 8
PARITIES = [
    [z * Y + h * X + y + q for y in range(0, X, 2) for z in range(Z_LO) for h in range(Y // X)]
    for q in range(2)
]
LINES = [[(z * X + x) * CORE + c for x in range(X)] for z in range(Z_HI) for c in range(CORE)]


def along_z(array, by):
    step = X * CORE
    pairs = [(i, (i + by * step) % (Z_HI * step)) for i in range(Z_HI * step)]
    return lax.ppermute(array, "row", pairs)


def other_core(array):
    return lax.ppermute(array, "row", [(i, i ^ 1) for i in range(Z_HI * X * CORE)])


def neighbour(array, by):
    pairs = [
        (z * Y + y, z * Y + (y + (by if y % 2 == 0 else -by)) % Y)
        for z in range(Z_LO)
        for y in range(Y)
    ]
    return lax.ppermute(array, "col", pairs)


def share(part, axis, groups=None):
    count = len(groups[0]) if groups else lax.axis_size(axis)
    copies = jnp.broadcast_to(part[None], (count,) + part.shape)
    return lax.all_to_all(copies, axis, 0, 0, axis_index_groups=groups)


def gather(noise, data):
    z = lax.axis_index("row") // (X * CORE)
    same = share(noise, "col", PARITIES)
    plane = jnp.zeros((Z_HI,) + data.shape, data.dtype)
    pieces = (data, along_z(data, -1), along_z(data, 2), along_z(data, 1))
    for by, piece in enumerate(pieces):
        plane = lax.dynamic_update_slice(plane, piece[None], ((z + by) % Z_HI, 0, 0))
    return lax.optimization_barrier((same, plane))


def log_total(scores, dim, axis):
    peak = jnp.max(scores, axis=dim)
    total = jnp.sum(jnp.exp(scores - jnp.expand_dims(peak, dim)), axis=dim)
    logs = share(peak + jnp.log(total), axis)
    whole = jnp.max(logs, axis=0)
    return whole + jnp.log(jnp.sum(jnp.exp(logs - whole[None]), axis=0))


def local(noise, data):
    rows, cols = noise.shape[0], data.shape[1]
    width = noise.shape[1] * lax.axis_size("col")
    rows_all = rows * lax.axis_size("row")
    cols_all = cols * lax.axis_size("col")
    core = lax.axis_index("row") % CORE

    odd = lax.axis_index("col") % 2

    same, plane = gather(noise, data)
    here = share(plane, "row", LINES)
    n = len(PARITIES[0]) // 2
    other = jnp.concatenate([neighbour(same[:n], 1), neighbour(same[n:], -1)])
    by_parity = [jnp.where(odd == 0, same, other), jnp.where(odd == 0, other, same)]
    noise_sq = sum(jnp.sum(part.astype(jnp.float32) ** 2, axis=(0, 2)) for part in by_parity)

    def half(which):
        size = noise.shape[1] // CORE
        part = [p[:, :, which * size : (which + 1) * size] for p in by_parity]
        part = [p.reshape((X // 2, -1) + p.shape[1:]) for p in part]
        return jnp.stack(part, axis=1).transpose(3, 0, 1, 2, 4).reshape(rows, -1)

    first, second = half(0), half(1)
    mine = jnp.where(core == 0, first, second)
    others = jnp.where(core == 0, second, first)
    here, _, kept, away = lax.optimization_barrier(
        (here, other, odd.astype(jnp.uint32), (1 - odd).astype(jnp.uint32))
    )
    there = other_core(here)
    sq = jnp.sum(here.astype(jnp.float32) ** 2, axis=(0, 1, 2))
    data_sq = sq + other_core(sq)
    cross = jnp.dot(mine, here.reshape(-1, cols), preferred_element_type=jnp.float32)
    cross += jnp.dot(others, there.reshape(-1, cols), preferred_element_type=jnp.float32)

    unit = 1.0 / (width * EPS)
    logits = cross * (2.0 * unit)
    row_first = -jnp.log(float(rows_all)) - log_total(
        logits - (data_sq * unit)[None, :], 1, "col"
    )
    col_first = -jnp.log(float(cols_all)) - log_total(logits + row_first[:, None], 0, "row")

    lift = 2.0**LIFT
    plan = lift * jnp.exp(logits + row_first[:, None] + col_first[None, :])
    by_col = jnp.ones((cols,), jnp.float32)
    for step in range(1, ITERS):
        part = jnp.sum(plan * by_col[None, :], axis=1)
        by_row = (lift / rows_all) / jnp.sum(share(part, "col"), axis=0)
        part = jnp.sum(plan * by_row[:, None], axis=0)
        by_col = (lift / cols_all) / jnp.sum(share(part, "row"), axis=0)
    row_potential = noise_sq / width + EPS * (row_first + jnp.log(by_row))
    col_potential = data_sq / width + EPS * (col_first + jnp.log(by_col))

    weights = (plan * ((rows_all / lift) * by_row)[:, None] * by_col[None, :]).astype(
        jnp.bfloat16
    )

    def features(parity):
        shape = (X // 2, 2, Z_HI, -1, cols)
        a = lax.dynamic_index_in_dim(here.reshape(shape), parity, 1, keepdims=False)
        b = lax.dynamic_index_in_dim(there.reshape(shape), parity, 1, keepdims=False)
        both = [jnp.where(core == 0, a, b), jnp.where(core == 0, b, a)]
        return jnp.stack(both, axis=2).reshape(X // 2, -1, cols)

    def terms(part):
        contract = (((1,), (1,)), ((), ()))
        return lax.dot_general(part, weights, contract, preferred_element_type=jnp.float32)

    sent = [terms(part).astype(jnp.bfloat16) for part in features(away)]
    got = [neighbour(part, by) for part, by in zip(sent, (1, -1))]
    sums = [
        (terms(own) + add).astype(jnp.bfloat16) for own, add in zip(features(kept), got)
    ]
    sums = jnp.stack(sums).reshape(len(PARITIES[0]), -1, rows)
    parts = lax.all_to_all(sums, "col", 0, 0, axis_index_groups=PARITIES)
    targets = jnp.sum(parts.astype(jnp.float32), axis=0).astype(jnp.bfloat16)
    return (targets, row_potential, col_potential)


def solution(mesh):
    placed = (P("row", "col"), P("row", "col"))
    return jax.shard_map(
        local,
        mesh=mesh,
        in_specs=placed,
        out_specs=(P("col", "row"), P("row"), P("col")),
        check_vma=False,
    )
```

```python
import jax
import jax.numpy as jnp
from jax import lax
from jax.sharding import PartitionSpec as P

ITERS = 4

EPS = 0.01
LIFT = 64

Z_HI, X, CORE = 4, 4, 2
Z_LO, Y = 2, 8
PARITIES = [
    [z * Y + h * X + y + q for y in range(0, X, 2) for z in range(Z_LO) for h in range(Y // X)]
    for q in range(2)
]
LINES = [[(z * X + x) * CORE + c for x in range(X)] for z in range(Z_HI) for c in range(CORE)]


def along_z(array, by):
    step = X * CORE
    pairs = [(i, (i + by * step) % (Z_HI * step)) for i in range(Z_HI * step)]
    return lax.ppermute(array, "row", pairs)


def other_core(array):
    return lax.ppermute(array, "row", [(i, i ^ 1) for i in range(Z_HI * X * CORE)])


def neighbour(array, by):
    pairs = [
        (z * Y + y, z * Y + (y + (by if y % 2 == 0 else -by)) % Y)
        for z in range(Z_LO)
        for y in range(Y)
    ]
    return lax.ppermute(array, "col", pairs)


def share(part, axis, groups=None):
    count = len(groups[0]) if groups else lax.axis_size(axis)
    copies = jnp.broadcast_to(part[None], (count,) + part.shape)
    return lax.all_to_all(copies, axis, 0, 0, axis_index_groups=groups)


def gather(noise, data):
    z = lax.axis_index("row") // (X * CORE)
    same = share(noise, "col", PARITIES)
    plane = jnp.zeros((Z_HI,) + data.shape, data.dtype)
    pieces = (data, along_z(data, -1), along_z(data, 2), along_z(data, 1))
    for by, piece in enumerate(pieces):
        plane = lax.dynamic_update_slice(plane, piece[None], ((z + by) % Z_HI, 0, 0))
    return lax.optimization_barrier((same, plane))


def log_total(scores, dim, axis):
    peak = jnp.max(scores, axis=dim)
    total = jnp.sum(jnp.exp(scores - jnp.expand_dims(peak, dim)), axis=dim)
    logs = share(peak + jnp.log(total), axis)
    whole = jnp.max(logs, axis=0)
    return whole + jnp.log(jnp.sum(jnp.exp(logs - whole[None]), axis=0))


def local(noise, data):
    rows, cols = noise.shape[0], data.shape[1]
    width = noise.shape[1] * lax.axis_size("col")
    rows_all = rows * lax.axis_size("row")
    cols_all = cols * lax.axis_size("col")
    core = lax.axis_index("row") % CORE

    odd = lax.axis_index("col") % 2

    same, plane = gather(noise, data)
    here = share(plane, "row", LINES)
    n = len(PARITIES[0]) // 2
    other = jnp.concatenate([neighbour(same[:n], 1), neighbour(same[n:], -1)])
    by_parity = [jnp.where(odd == 0, same, other), jnp.where(odd == 0, other, same)]
    noise_sq = sum(jnp.sum(part.astype(jnp.float32) ** 2, axis=(0, 2)) for part in by_parity)

    def half(which):
        size = noise.shape[1] // CORE
        part = [p[:, :, which * size : (which + 1) * size] for p in by_parity]
        part = [p.reshape((X // 2, -1) + p.shape[1:]) for p in part]
        return jnp.stack(part, axis=1).transpose(3, 0, 1, 2, 4).reshape(rows, -1)

    first, second = half(0), half(1)
    mine = jnp.where(core == 0, first, second)
    others = jnp.where(core == 0, second, first)
    here, _, kept, away = lax.optimization_barrier(
        (here, noise_sq, odd.astype(jnp.uint32), (1 - odd).astype(jnp.uint32))
    )
    there = other_core(here)
    sq = jnp.sum(here.astype(jnp.float32) ** 2, axis=(0, 1, 2))
    data_sq = sq + other_core(sq)
    cross = jnp.dot(mine, here.reshape(-1, cols), preferred_element_type=jnp.float32)
    cross += jnp.dot(others, there.reshape(-1, cols), preferred_element_type=jnp.float32)

    unit = 1.0 / (width * EPS)
    logits = cross * (2.0 * unit)
    row_first = -jnp.log(float(rows_all)) - log_total(
        logits - (data_sq * unit)[None, :], 1, "col"
    )
    col_first = -jnp.log(float(cols_all)) - log_total(logits + row_first[:, None], 0, "row")

    lift = 2.0**LIFT
    plan = lift * jnp.exp(logits + row_first[:, None] + col_first[None, :])
    by_col = jnp.ones((cols,), jnp.float32)
    for step in range(1, ITERS):
        part = jnp.sum(plan * by_col[None, :], axis=1)
        by_row = (lift / rows_all) / jnp.sum(share(part, "col"), axis=0)
        part = jnp.sum(plan * by_row[:, None], axis=0)
        by_col = (lift / cols_all) / jnp.sum(share(part, "row"), axis=0)
    row_potential = noise_sq / width + EPS * (row_first + jnp.log(by_row))
    col_potential = data_sq / width + EPS * (col_first + jnp.log(by_col))

    weights = (plan * ((rows_all / lift) * by_row)[:, None] * by_col[None, :]).astype(
        jnp.bfloat16
    )

    def features(parity):
        shape = (X // 2, 2, Z_HI, -1, cols)
        a = lax.dynamic_index_in_dim(here.reshape(shape), parity, 1, keepdims=False)
        b = lax.dynamic_index_in_dim(there.reshape(shape), parity, 1, keepdims=False)
        both = [jnp.where(core == 0, a, b), jnp.where(core == 0, b, a)]
        return jnp.stack(both, axis=2).reshape(X // 2, -1, cols)

    def terms(part):
        contract = (((1,), (1,)), ((), ()))
        return lax.dot_general(part, weights, contract, preferred_element_type=jnp.float32)

    sent = [terms(part).astype(jnp.bfloat16) for part in features(away)]
    got = [neighbour(part, by) for part, by in zip(sent, (1, -1))]
    sums = [
        (terms(own) + add).astype(jnp.bfloat16) for own, add in zip(features(kept), got)
    ]
    sums = jnp.stack(sums).reshape(len(PARITIES[0]), -1, rows)
    parts = lax.all_to_all(sums, "col", 0, 0, axis_index_groups=PARITIES)
    targets = jnp.sum(parts.astype(jnp.float32), axis=0).astype(jnp.bfloat16)
    return (targets, row_potential, col_potential)


def solution(mesh):
    placed = (P("row", "col"), P("row", "col"))
    return jax.shard_map(
        local,
        mesh=mesh,
        in_specs=placed,
        out_specs=(P("col", "row"), P("row"), P("col")),
        check_vma=False,
    )
```

```python
import jax
import jax.numpy as jnp
from jax import lax
from jax.sharding import PartitionSpec as P

ITERS = 4

EPS = 0.01
LIFT = 64

Z_HI, X, CORE = 4, 4, 2
Z_LO, Y = 2, 8
PARITIES = [
    [z * Y + h * X + y + q for y in range(0, X, 2) for z in range(Z_LO) for h in range(Y // X)]
    for q in range(2)
]
LINES = [[(z * X + x) * CORE + c for x in range(X)] for z in range(Z_HI) for c in range(CORE)]


def along_z(array, by):
    step = X * CORE
    pairs = [(i, (i + by * step) % (Z_HI * step)) for i in range(Z_HI * step)]
    return lax.ppermute(array, "row", pairs)


def other_core(array):
    return lax.ppermute(array, "row", [(i, i ^ 1) for i in range(Z_HI * X * CORE)])


def neighbour(array, by):
    pairs = [
        (z * Y + y, z * Y + (y + (by if y % 2 == 0 else -by)) % Y)
        for z in range(Z_LO)
        for y in range(Y)
    ]
    return lax.ppermute(array, "col", pairs)


def share(part, axis, groups=None):
    count = len(groups[0]) if groups else lax.axis_size(axis)
    copies = jnp.broadcast_to(part[None], (count,) + part.shape)
    return lax.all_to_all(copies, axis, 0, 0, axis_index_groups=groups)


def gather(noise, data):
    z = lax.axis_index("row") // (X * CORE)
    same = share(noise, "col", PARITIES)
    plane = jnp.zeros((Z_HI,) + data.shape, data.dtype)
    for by in (2, 3, 1, 0):
        piece = along_z(data, -by) if by else data
        plane = lax.dynamic_update_slice(plane, piece[None], ((z + by) % Z_HI, 0, 0))
    return lax.optimization_barrier((same, plane))


def log_total(scores, dim, axis):
    peak = jnp.max(scores, axis=dim)
    total = jnp.sum(jnp.exp(scores - jnp.expand_dims(peak, dim)), axis=dim)
    logs = share(peak + jnp.log(total), axis)
    whole = jnp.max(logs, axis=0)
    return whole + jnp.log(jnp.sum(jnp.exp(logs - whole[None]), axis=0))


def local(noise, data):
    rows, cols = noise.shape[0], data.shape[1]
    width = noise.shape[1] * lax.axis_size("col")
    rows_all = rows * lax.axis_size("row")
    cols_all = cols * lax.axis_size("col")
    core = lax.axis_index("row") % CORE

    odd = lax.axis_index("col") % 2

    same, plane = gather(noise, data)
    here = share(plane, "row", LINES)
    n = len(PARITIES[0]) // 2
    other = jnp.concatenate([neighbour(same[:n], 1), neighbour(same[n:], -1)])
    by_parity = [jnp.where(odd == 0, same, other), jnp.where(odd == 0, other, same)]
    noise_sq = sum(jnp.sum(part.astype(jnp.float32) ** 2, axis=(0, 2)) for part in by_parity)

    def half(which):
        size = noise.shape[1] // CORE
        part = [p[:, :, which * size : (which + 1) * size] for p in by_parity]
        part = [p.reshape((X // 2, -1) + p.shape[1:]) for p in part]
        return jnp.stack(part, axis=1).transpose(3, 0, 1, 2, 4).reshape(rows, -1)

    first, second = half(0), half(1)
    mine = jnp.where(core == 0, first, second)
    others = jnp.where(core == 0, second, first)
    here, _, kept, away = lax.optimization_barrier(
        (here, noise_sq, odd.astype(jnp.uint32), (1 - odd).astype(jnp.uint32))
    )
    there = other_core(here)
    sq = jnp.sum(here.astype(jnp.float32) ** 2, axis=(0, 1, 2))
    data_sq = sq + other_core(sq)
    cross = jnp.dot(mine, here.reshape(-1, cols), preferred_element_type=jnp.float32)
    cross += jnp.dot(others, there.reshape(-1, cols), preferred_element_type=jnp.float32)

    unit = 1.0 / (width * EPS)
    logits = cross * (2.0 * unit)
    row_first = -jnp.log(float(rows_all)) - log_total(
        logits - (data_sq * unit)[None, :], 1, "col"
    )
    col_first = -jnp.log(float(cols_all)) - log_total(logits + row_first[:, None], 0, "row")

    lift = 2.0**LIFT
    plan = lift * jnp.exp(logits + row_first[:, None] + col_first[None, :])
    by_col = jnp.ones((cols,), jnp.float32)
    for step in range(1, ITERS):
        part = jnp.sum(plan * by_col[None, :], axis=1)
        by_row = (lift / rows_all) / jnp.sum(share(part, "col"), axis=0)
        part = jnp.sum(plan * by_row[:, None], axis=0)
        by_col = (lift / cols_all) / jnp.sum(share(part, "row"), axis=0)
    row_potential = noise_sq / width + EPS * (row_first + jnp.log(by_row))
    col_potential = data_sq / width + EPS * (col_first + jnp.log(by_col))

    weights = (plan * ((rows_all / lift) * by_row)[:, None] * by_col[None, :]).astype(
        jnp.bfloat16
    )

    def features(parity):
        shape = (X // 2, 2, Z_HI, -1, cols)
        a = lax.dynamic_index_in_dim(here.reshape(shape), parity, 1, keepdims=False)
        b = lax.dynamic_index_in_dim(there.reshape(shape), parity, 1, keepdims=False)
        both = [jnp.where(core == 0, a, b), jnp.where(core == 0, b, a)]
        return jnp.stack(both, axis=2).reshape(X // 2, -1, cols)

    def terms(part):
        contract = (((1,), (1,)), ((), ()))
        return lax.dot_general(part, weights, contract, preferred_element_type=jnp.float32)

    sent = [terms(part).astype(jnp.bfloat16) for part in features(away)]
    got = [neighbour(part, by) for part, by in zip(sent, (1, -1))]
    sums = [
        (terms(own) + add).astype(jnp.bfloat16) for own, add in zip(features(kept), got)
    ]
    sums = jnp.stack(sums).reshape(len(PARITIES[0]), -1, rows)
    parts = lax.all_to_all(sums, "col", 0, 0, axis_index_groups=PARITIES)
    targets = jnp.sum(parts.astype(jnp.float32), axis=0).astype(jnp.bfloat16)
    return (targets, row_potential, col_potential)


def solution(mesh):
    placed = (P("row", "col"), P("row", "col"))
    return jax.shard_map(
        local,
        mesh=mesh,
        in_specs=placed,
        out_specs=(P("col", "row"), P("row"), P("col")),
        check_vma=False,
    )
```

```python
import jax
import jax.numpy as jnp
from jax import lax
from jax.sharding import PartitionSpec as P

ITERS = 4

EPS = 0.01
LIFT = 64

Z_HI, X, CORE = 4, 4, 2
Z_LO, Y = 2, 8
PARITIES = [
    [z * Y + h * X + y + q for y in range(0, X, 2) for z in range(Z_LO) for h in range(Y // X)]
    for q in range(2)
]
LINES = [[(z * X + x) * CORE + c for x in range(X)] for z in range(Z_HI) for c in range(CORE)]


def along_z(array, by):
    step = X * CORE
    pairs = [(i, (i + by * step) % (Z_HI * step)) for i in range(Z_HI * step)]
    return lax.ppermute(array, "row", pairs)


def other_core(array):
    return lax.ppermute(array, "row", [(i, i ^ 1) for i in range(Z_HI * X * CORE)])


def neighbour(array, by):
    pairs = [
        (z * Y + y, z * Y + (y + (by if y % 2 == 0 else -by)) % Y)
        for z in range(Z_LO)
        for y in range(Y)
    ]
    return lax.ppermute(array, "col", pairs)


def share(part, axis, groups=None):
    count = len(groups[0]) if groups else lax.axis_size(axis)
    copies = jnp.broadcast_to(part[None], (count,) + part.shape)
    return lax.all_to_all(copies, axis, 0, 0, axis_index_groups=groups)


def gather(noise, data):
    z = lax.axis_index("row") // (X * CORE)
    same = share(noise, "col", PARITIES)
    plane = jnp.zeros((Z_HI,) + data.shape, data.dtype)
    for by in (2, 3, 1, 0):
        piece = along_z(data, -by) if by else data
        plane = lax.dynamic_update_slice(plane, piece[None], ((z + by) % Z_HI, 0, 0))
    return lax.optimization_barrier((same, plane))


def log_total(scores, dim, axis):
    peak = jnp.max(scores, axis=dim)
    total = jnp.sum(jnp.exp(scores - jnp.expand_dims(peak, dim)), axis=dim)
    logs = share(peak + jnp.log(total), axis)
    whole = jnp.max(logs, axis=0)
    return whole + jnp.log(jnp.sum(jnp.exp(logs - whole[None]), axis=0))


def local(noise, data):
    rows, cols = noise.shape[0], data.shape[1]
    width = noise.shape[1] * lax.axis_size("col")
    rows_all = rows * lax.axis_size("row")
    cols_all = cols * lax.axis_size("col")
    core = lax.axis_index("row") % CORE

    odd = lax.axis_index("col") % 2

    same, plane = gather(noise, data)
    here = share(plane, "row", LINES)
    n = len(PARITIES[0]) // 2
    other = jnp.concatenate([neighbour(same[:n], 1), neighbour(same[n:], -1)])
    by_parity = [jnp.where(odd == 0, same, other), jnp.where(odd == 0, other, same)]
    noise_sq = sum(jnp.sum(part.astype(jnp.float32) ** 2, axis=(0, 2)) for part in by_parity)

    def half(which):
        size = noise.shape[1] // CORE
        part = [p[:, :, which * size : (which + 1) * size] for p in by_parity]
        part = [p.reshape((X // 2, -1) + p.shape[1:]) for p in part]
        return jnp.stack(part, axis=1).transpose(3, 0, 1, 2, 4).reshape(rows, -1)

    first, second = half(0), half(1)
    mine = jnp.where(core == 0, first, second)
    others = jnp.where(core == 0, second, first)
    here, _, kept, away = lax.optimization_barrier(
        (here, noise_sq, odd.astype(jnp.uint32), (1 - odd).astype(jnp.uint32))
    )
    there = other_core(here)
    sq = jnp.sum(here.astype(jnp.float32) ** 2, axis=(0, 1, 2))
    data_sq = sq + other_core(sq)
    cross = jnp.dot(mine, here.reshape(-1, cols), preferred_element_type=jnp.float32)
    cross += jnp.dot(others, there.reshape(-1, cols), preferred_element_type=jnp.float32)

    unit = 1.0 / (width * EPS)
    logits = cross * (2.0 * unit)
    row_first = -jnp.log(float(rows_all)) - log_total(
        logits - (data_sq * unit)[None, :], 1, "col"
    )
    col_first = -jnp.log(float(cols_all)) - log_total(logits + row_first[:, None], 0, "row")

    lift = 2.0**LIFT
    plan = lift * jnp.exp(logits + row_first[:, None] + col_first[None, :])
    by_col = jnp.ones((cols,), jnp.float32)
    for step in range(1, ITERS):
        part = jnp.sum(plan * by_col[None, :], axis=1)
        by_row = (lift / rows_all) / jnp.sum(share(part, "col"), axis=0)
        part = jnp.sum(plan * by_row[:, None], axis=0)
        by_col = (lift / cols_all) / jnp.sum(share(part, "row"), axis=0)
    weights = (plan * ((rows_all / lift) * by_row)[:, None] * by_col[None, :]).astype(
        jnp.bfloat16
    )

    weights, by_row, by_col = lax.optimization_barrier((weights, by_row, by_col))
    row_potential = noise_sq / width + EPS * (row_first + jnp.log(by_row))
    col_potential = data_sq / width + EPS * (col_first + jnp.log(by_col))

    def features(parity):
        shape = (X // 2, 2, Z_HI, -1, cols)
        a = lax.dynamic_index_in_dim(here.reshape(shape), parity, 1, keepdims=False)
        b = lax.dynamic_index_in_dim(there.reshape(shape), parity, 1, keepdims=False)
        both = [jnp.where(core == 0, a, b), jnp.where(core == 0, b, a)]
        return jnp.stack(both, axis=2).reshape(X // 2, -1, cols)

    def terms(part):
        contract = (((1,), (1,)), ((), ()))
        return lax.dot_general(part, weights, contract, preferred_element_type=jnp.float32)

    sent = [terms(part).astype(jnp.bfloat16) for part in features(away)]
    got = [neighbour(part, by) for part, by in zip(sent, (1, -1))]
    got, row_potential, col_potential = lax.optimization_barrier(
        (got, row_potential, col_potential)
    )
    sums = [
        (terms(own) + add).astype(jnp.bfloat16) for own, add in zip(features(kept), got)
    ]
    sums = jnp.stack(sums).reshape(len(PARITIES[0]), -1, rows)
    parts = lax.all_to_all(sums, "col", 0, 0, axis_index_groups=PARITIES)
    targets = jnp.sum(parts.astype(jnp.float32), axis=0).astype(jnp.bfloat16)
    return (targets, row_potential, col_potential)


def solution(mesh):
    placed = (P("row", "col"), P("row", "col"))
    return jax.shard_map(
        local,
        mesh=mesh,
        in_specs=placed,
        out_specs=(P("col", "row"), P("row"), P("col")),
        check_vma=False,
    )
```
